256 devices in a mesh: row: 32 (over z, x_lo, core), col: 8 (over x_hi, y).
Axes of the slice: x: 4 (x_hi: 2, x_lo: 2; x = x_hi * 2 + x_lo), y: 4, z: 8, core: 2. Of those that a mesh axis runs over, the one named last changes fastest.
Arguments:
- queries: bfloat16 [1, 128, 128, 1536], P(None, 'row', 'col'), may hold values from -180 to 180
- key_tokens: bfloat16 [1, 128, 128, 1536], P(None, 'row', 'col'), may hold values from -4 to 4
- values: bfloat16 [1, 128, 128, 1536], P(None, 'row', 'col'), may hold values from -6 to 6
- position_bias: float32 [24, 49], replicated, may hold values from -4 to 4
- out_weight: bfloat16 [1536, 1536], P('col', 'row'), may hold values from -0.15625 to 0.15625
Outputs:
- projected: bfloat16 [1, 128, 128, 1536], P(None, 'row', 'col')
The draws below stay inside these ranges and needn't reach their ends.
All inputs are finite; a program needn't handle non-finite values.
Results may differ from the reference program's by a relative error of at most 0.0057.
Values may be sent and summed in bfloat16 or wider, within the bound.
No kernel may reach another device: no remote copies, remote signals or barrier semaphores. Data moves between devices by JAX's collectives and lax.ppermute only.
A program may use at most 64 MiB of HBM per device.

```python
import math
from functools import partial
import jax
import jax.numpy as jnp
from jax import lax

D = 1536
HEADS = 24
HEAD_DIM = 64
IMAGES = 1
IMG_H = 128
IMG_W = 128


def drawn_pair(key):
    shape = (IMAGES, IMG_H, IMG_W, D)
    normal_keys = jnp.clip(jax.random.normal(jax.random.fold_in(key, 11), shape, jnp.float32), -4.0, 4.0)
    normal_queries = jnp.clip(jax.random.normal(jax.random.fold_in(key, 12), shape, jnp.float32), -4.0, 4.0)
    return (normal_queries, normal_keys)


def draw_queries(key, part):
    return drawn_pair(key)[0].astype(jnp.bfloat16)


def draw_key_tokens(key, part):
    return drawn_pair(key)[1].astype(jnp.bfloat16)


def levels(key, shape, cuts, low, largest):
    factor_of = 1.0
    for position, blocks in cuts:
        heights = jax.random.uniform(jax.random.fold_in(jax.random.fold_in(key, 6), position), (blocks,), jnp.float32, low / len(cuts), largest / len(cuts))
        factor_of = factor_of * jnp.repeat(jnp.exp(heights), shape[position] // blocks).reshape((-1,) + (1,) * (len(shape) - 1 - position))
    return factor_of


def bell_draw(key, shape, width, most, pieces=(), kind=jnp.bfloat16):
    factor_of = levels(key, shape, pieces, -0.22, 0.18) if pieces else 1.0
    values = jax.random.normal(key, shape, jnp.float32) * width * factor_of
    return jnp.minimum(jnp.maximum(values, -most), most).astype(kind)


def setup_inputs(seed: int = 0) -> dict:
    seeds = jax.random.split(jax.random.key(seed), 6)
    return {
        "queries": draw_queries(jax.random.fold_in(seeds[5], 71), 0),
        "key_tokens": draw_key_tokens(jax.random.fold_in(seeds[5], 71), 0),
        "values": bell_draw(seeds[2], (IMAGES, IMG_H, IMG_W, D), 1.0, 6.0, ((1, 32), (2, 8))),
        "position_bias": bell_draw(seeds[3], (HEADS, 49), 1.0, 4.0, (), jnp.float32),
        "out_weight": bell_draw(seeds[4], (D, D), D ** -0.5, 0.15625, ((0, 8), (1, 32))),
    }


def one_image(items, position_bias, out_weight):
    query_img, key_img, value_img = items
    height = query_img.shape[0]
    breadth = query_img.shape[1]
    key_pad = jnp.pad(key_img, ((3, 3), (3, 3), (0, 0)))
    value_pad = jnp.pad(value_img, ((3, 3), (3, 3), (0, 0)))
    query_heads = query_img.astype(jnp.float32).reshape(height, breadth, HEADS, HEAD_DIM)
    row_pos = jnp.arange(height)
    col_pos = jnp.arange(breadth)
    score_scale = 1.0 / math.sqrt(HEAD_DIM)
    score_list = []
    for row_off in range(7):
        rows_inside = (row_pos + row_off - 3 >= 0) & (row_pos + row_off - 3 < height)
        for col_off in range(7):
            cols_inside = (col_pos + col_off - 3 >= 0) & (col_pos + col_off - 3 < breadth)
            shifted = key_pad[row_off:row_off + height, col_off:col_off + breadth].astype(jnp.float32)
            shifted = shifted.reshape(height, breadth, HEADS, HEAD_DIM)
            score = jnp.einsum('yxhd,yxhd->yxh', query_heads, shifted) * score_scale
            score = score + position_bias[:, row_off * 7 + col_off][None, None, :]
            inside = rows_inside[:, None] & cols_inside[None, :]
            score_list.append(jnp.where(inside[:, :, None], score, -jnp.inf))
    scores = jnp.stack(score_list, -1)
    attention = jax.nn.softmax(scores, axis=-1).astype(jnp.bfloat16)
    total = jnp.zeros((height, breadth, HEADS, HEAD_DIM), jnp.float32)
    for row_off in range(7):
        for col_off in range(7):
            shifted = value_pad[row_off:row_off + height, col_off:col_off + breadth].astype(jnp.float32)
            shifted = shifted.reshape(height, breadth, HEADS, HEAD_DIM)
            weight_one = attention[:, :, :, row_off * 7 + col_off].astype(jnp.float32)
            total = total + weight_one[..., None] * shifted
    mixed = total.reshape(height * breadth, D).astype(jnp.bfloat16)
    result = jnp.dot(mixed, out_weight, preferred_element_type=jnp.float32)
    return result.astype(jnp.bfloat16).reshape(height, breadth, D)

def reference(queries, key_tokens, values, position_bias, out_weight):
    per_image = partial(one_image, position_bias=position_bias, out_weight=out_weight)
    return lax.map(per_image, (queries, key_tokens, values))
```

```python
import jax
import jax.numpy as jnp
import numpy as np
from jax import lax
from jax.experimental import pallas as pl
from jax.experimental.pallas import tpu as pltpu
from jax.sharding import Mesh, PartitionSpec as P

VM = pl.BlockSpec(memory_space=pltpu.VMEM)
SM = pl.BlockSpec(memory_space=pltpu.SMEM)
BF = jnp.bfloat16
F32 = jnp.float32
NT = (((1,), (1,)), ((), ()))


def col_pick():
    pick = np.zeros((64, 160), np.float32)
    for side, first in ((0, 0), (1, 13)):
        for r in range(10):
            for j in range(3):
                x = first + j
                if r < 3:
                    source = 64 + r * 16 + x
                elif r < 7:
                    source = (r - 3) * 16 + x
                else:
                    source = 112 + (r - 7) * 16 + x
                pick[side * 32 + r * 3 + j, source] = 1.0
    return pick


def pack_kernel(pick_ref, k_ref, v_ref, top_ref, bot_ref, left_ref, right_ref):
    pick = pick_ref[...]
    for n, own in ((0, k_ref), (1, v_ref)):
        tokens = jnp.concatenate(
            [own[...], top_ref[n * 48 : n * 48 + 48, :], bot_ref[n * 48 : n * 48 + 48, :]], 0
        )
        got = jnp.dot(pick, tokens, preferred_element_type=F32).astype(BF)
        left_ref[n * 32 : n * 32 + 32, :] = got[:32]
        right_ref[n * 32 : n * 32 + 32, :] = got[32:]


def attention_kernel(
    place_ref, q_ref, k_ref, v_ref, top_ref, bot_ref, left_ref, right_ref, bias_ref, o_ref
):
    heads = bias_ref.shape[0]
    shape = (64, 256)
    i = lax.broadcasted_iota(jnp.int32, shape, 0)
    j = lax.broadcasted_iota(jnp.int32, shape, 1)
    y, x = i >> 4, i & 15
    side = j & 31
    side_row = ((side * 171) >> 9) - 3
    side_col = side - (side_row + 3) * 3
    ky = jnp.where(
        j < 64,
        j >> 4,
        jnp.where(j < 112, (j >> 4) - 7, jnp.where(j < 160, (j >> 4) - 3, side_row)),
    )
    kx = jnp.where(j < 160, j & 15, jnp.where(j < 192, side_col - 3, side_col + 16))
    dy, dx = ky - y + 3, kx - x + 3
    gy, gx = ky + place_ref[0], kx + place_ref[1]
    inside = (dy >= 0) & (dy < 7) & (dx >= 0) & (dx < 7)
    inside = inside & (gy >= 0) & (gy < place_ref[2]) & (gx >= 0) & (gx < place_ref[3])
    inside = inside & ((j < 160) | (side < 30)) & (j < 224)
    code = jnp.where(inside, dy * 7 + dx, 127)
    code_low, code_high = code[:, :128], code[:, 128:]
    low = lax.broadcasted_iota(jnp.int32, (64, 128), 1) < 64
    zeros = jnp.zeros((32, 128), BF)
    none = jnp.zeros((64, 128), BF)

    for pair in range(heads // 2):
        c = slice(pair * 128, pair * 128 + 128)
        q = q_ref[:, c]
        q2 = jnp.concatenate([jnp.where(low, q, none), jnp.where(low, none, q)], 0)
        keys = jnp.concatenate(
            [k_ref[:, c], top_ref[:48, c], bot_ref[:48, c], left_ref[:32, c], right_ref[:32, c], zeros], 0
        )
        vals = jnp.concatenate(
            [v_ref[:, c], top_ref[48:, c], bot_ref[48:, c], left_ref[32:, c], right_ref[32:, c], zeros], 0
        )
        s = lax.dot_general(q2, keys, NT, preferred_element_type=F32)
        bias = []
        for h in (2 * pair, 2 * pair + 1):
            row = jnp.broadcast_to(bias_ref[h : h + 1, :], (64, 128))
            bias.append(
                jnp.concatenate(
                    [
                        jnp.take_along_axis(row, code_low, axis=1, mode="promise_in_bounds"),
                        jnp.take_along_axis(row, code_high, axis=1, mode="promise_in_bounds"),
                    ],
                    1,
                )
            )
        s = s * 0.125 + jnp.concatenate(bias, 0)
        e = jnp.exp(s - jnp.max(s, 1, keepdims=True))
        p = (e * (1.0 / jnp.sum(e, 1, keepdims=True))).astype(BF)
        o = jnp.dot(p, vals, preferred_element_type=F32)
        o_ref[:, c] = jnp.where(low, o[:64], o[64:]).astype(BF)


def project_kernel(core_ref, mine_ref, other_ref, w_ref, keep_ref, send_ref):
    mixed = jnp.concatenate([mine_ref[...], other_ref[...]], 0)
    total = None
    for xh in range(2):
        for y in range(4):
            block = xh * 4 + y
            feats = mixed[:, block * 192 : block * 192 + 192]
            parts = []
            for z in range(8):
                for xl in range(2):
                    w = w_ref[xh, xl, y, z]
                    tail = w[48:]
                    tail = jnp.concatenate([tail[:, :64], tail[:, 64:]], 0)
                    parts.append(jnp.concatenate([w[:48], tail], 1))
            wt = jnp.concatenate(parts, 0)
            term = lax.dot_general(feats, wt, NT, preferred_element_type=F32)
            total = term if total is None else total + term
    out = total.astype(BF)
    keep_ref[...] = out[:64]
    send_ref[...] = out[64:]


def assemble_kernel(core_ref, mine_ref, other_ref, o_ref):
    first = core_ref[0] == 0
    mine, other = mine_ref[...].astype(F32), other_ref[...].astype(F32)
    a = jnp.where(first, mine, other)
    b = jnp.where(first, other, mine)
    pieces = []
    for n in range(16):
        pieces += [a[:, n * 48 : n * 48 + 48], b[:, n * 48 : n * 48 + 48]]
    o_ref[...] = jnp.concatenate(pieces, 1).astype(BF)


def call(kernel, outs, n_in, smem=(), limit=48):
    return pl.pallas_call(
        kernel,
        out_shape=outs,
        in_specs=[SM if k in smem else VM for k in range(n_in)],
        out_specs=VM if isinstance(outs, jax.ShapeDtypeStruct) else tuple(VM for _ in outs),
        compiler_params=pltpu.CompilerParams(vmem_limit_bytes=limit * 1024 * 1024),
    )


def shards(queries, key_tokens, values, position_bias, out_weight):
    width = queries.shape[3]
    rows, cols = ("z", "xl", "core"), ("xh", "y")
    nr, nc = lax.axis_size(rows), lax.axis_size(cols)
    r, c = lax.axis_index(rows), lax.axis_index(cols)
    core = lax.axis_index("core")

    wt = out_weight.T
    packed = jnp.concatenate([wt[:, :128], jnp.concatenate([wt[:24, 128:], wt[24:, 128:]], 1)], 0)
    along_z = lax.all_to_all(jnp.broadcast_to(packed[None], (8, 72, 128)), "z", 0, 0, tiled=True)
    plane = lax.all_to_all(
        jnp.broadcast_to(along_z[None], (16, 8, 72, 128)), ("xh", "xl", "y"), 0, 0, tiled=True
    )
    weights = plane.reshape(2, 2, 4, 8, 72, 128)

    down = [(n, n + 1) for n in range(nr - 1)]
    up = [(n + 1, n) for n in range(nr - 1)]
    right = [(n, n + 1) for n in range(nc - 1)]
    left = [(n + 1, n) for n in range(nc - 1)]
    k, v, q = (a.reshape(64, width) for a in (key_tokens, values, queries))
    top = lax.ppermute(jnp.concatenate([k[16:], v[16:]], 0), rows, down)
    bot = lax.ppermute(jnp.concatenate([k[:48], v[:48]], 0), rows, up)
    side = jax.ShapeDtypeStruct((64, width), BF)
    to_left, to_right = call(pack_kernel, (side, side), 5)(jnp.asarray(col_pick(), BF), k, v, top, bot)
    from_left = lax.ppermute(to_right, cols, right)
    from_right = lax.ppermute(to_left, cols, left)

    place = jnp.stack([r * 4, c * 16, nr * 4, nc * 16]).astype(jnp.int32)
    bias = jnp.pad(position_bias, ((0, 0), (0, 128 - 49)), constant_values=-jnp.inf)
    mixed = call(attention_kernel, side, 9, smem=(0,))(
        place, q, k, v, top, bot, from_left, from_right, bias
    )
    swap = [(0, 1), (1, 0)]
    other = lax.ppermute(mixed, "core", swap)
    half = jax.ShapeDtypeStruct((64, width // 2), BF)
    core_id = core.astype(jnp.int32).reshape(1)
    keep, send = call(project_kernel, (half, half), 4, smem=(0,))(core_id, mixed, other, weights)
    got = lax.ppermute(send, "core", swap)
    out = call(assemble_kernel, side, 3, smem=(0,))(core_id, keep, got)
    return out.reshape(queries.shape)


def solution(mesh):
    fine = Mesh(mesh.devices.reshape(8, 2, 2, 2, 4), ("z", "xl", "core", "xh", "y"))
    rows, cols = ("z", "xl", "core"), ("xh", "y")
    tokens = P(None, rows, cols, None)
    return jax.shard_map(
        shards,
        mesh=fine,
        in_specs=(tokens, tokens, tokens, P(), P(cols, rows)),
        out_specs=tokens,
        check_vma=False,
    )
```

```python
import jax
import jax.numpy as jnp
import numpy as np
from jax import lax
from jax.experimental import pallas as pl
from jax.experimental.pallas import tpu as pltpu
from jax.sharding import Mesh, PartitionSpec as P

VM = pl.BlockSpec(memory_space=pltpu.VMEM)
SM = pl.BlockSpec(memory_space=pltpu.SMEM)
BF = jnp.bfloat16
F32 = jnp.float32
NT = (((1,), (1,)), ((), ()))


def col_pick():
    pick = np.zeros((64, 160), np.float32)
    for side, first in ((0, 0), (1, 13)):
        for r in range(10):
            for j in range(3):
                x = first + j
                if r < 3:
                    source = 64 + r * 16 + x
                elif r < 7:
                    source = (r - 3) * 16 + x
                else:
                    source = 112 + (r - 7) * 16 + x
                pick[side * 32 + r * 3 + j, source] = 1.0
    return pick


def pack_kernel(pick_ref, k_ref, v_ref, top_ref, bot_ref, left_ref, right_ref):
    pick = pick_ref[...]
    for n, own in ((0, k_ref), (1, v_ref)):
        tokens = jnp.concatenate(
            [own[...], top_ref[n * 48 : n * 48 + 48, :], bot_ref[n * 48 : n * 48 + 48, :]], 0
        )
        got = jnp.dot(pick, tokens, preferred_element_type=F32).astype(BF)
        left_ref[n * 32 : n * 32 + 32, :] = got[:32]
        right_ref[n * 32 : n * 32 + 32, :] = got[32:]


def attention_kernel(
    place_ref, q_ref, k_ref, v_ref, top_ref, bot_ref, left_ref, right_ref, bias_ref, o_ref
):
    heads = bias_ref.shape[0]
    shape = (64, 256)
    i = lax.broadcasted_iota(jnp.int32, shape, 0)
    j = lax.broadcasted_iota(jnp.int32, shape, 1)
    y, x = i >> 4, i & 15
    side = j & 31
    side_row = ((side * 171) >> 9) - 3
    side_col = side - (side_row + 3) * 3
    ky = jnp.where(
        j < 64,
        j >> 4,
        jnp.where(j < 112, (j >> 4) - 7, jnp.where(j < 160, (j >> 4) - 3, side_row)),
    )
    kx = jnp.where(j < 160, j & 15, jnp.where(j < 192, side_col - 3, side_col + 16))
    dy, dx = ky - y + 3, kx - x + 3
    gy, gx = ky + place_ref[0], kx + place_ref[1]
    inside = (dy >= 0) & (dy < 7) & (dx >= 0) & (dx < 7)
    inside = inside & (gy >= 0) & (gy < place_ref[2]) & (gx >= 0) & (gx < place_ref[3])
    inside = inside & ((j < 160) | (side < 30)) & (j < 224)
    code = jnp.where(inside, dy * 7 + dx, 127)
    code_low, code_high = code[:, :128], code[:, 128:]
    low = lax.broadcasted_iota(jnp.int32, (64, 128), 1) < 64
    zeros = jnp.zeros((32, 128), BF)
    none = jnp.zeros((64, 128), BF)

    for pair in range(heads // 2):
        c = slice(pair * 128, pair * 128 + 128)
        q = q_ref[:, c]
        q2 = jnp.concatenate([jnp.where(low, q, none), jnp.where(low, none, q)], 0)
        keys = jnp.concatenate(
            [k_ref[:, c], top_ref[:48, c], bot_ref[:48, c], left_ref[:32, c], right_ref[:32, c], zeros], 0
        )
        vals = jnp.concatenate(
            [v_ref[:, c], top_ref[48:, c], bot_ref[48:, c], left_ref[32:, c], right_ref[32:, c], zeros], 0
        )
        s = lax.dot_general(q2, keys, NT, preferred_element_type=F32)
        bias = []
        for h in (2 * pair, 2 * pair + 1):
            row = jnp.broadcast_to(bias_ref[h : h + 1, :], (64, 128))
            bias.append(
                jnp.concatenate(
                    [
                        jnp.take_along_axis(row, code_low, axis=1, mode="promise_in_bounds"),
                        jnp.take_along_axis(row, code_high, axis=1, mode="promise_in_bounds"),
                    ],
                    1,
                )
            )
        s = s * 0.125 + jnp.concatenate(bias, 0)
        e = jnp.exp(s - jnp.max(s, 1, keepdims=True))
        p = (e * (1.0 / jnp.sum(e, 1, keepdims=True))).astype(BF)
        o = jnp.dot(p, vals, preferred_element_type=F32)
        o_ref[:, c] = jnp.where(low, o[:64], o[64:]).astype(BF)


def project_kernel(a_ref, b_ref, c_ref, d_ref, w_ref, keep_ref, send_ref):
    mixed = jnp.concatenate([a_ref[...], b_ref[...], c_ref[...], d_ref[...]], 0)
    total = None
    for xh in range(2):
        for y in range(4):
            block = xh * 4 + y
            feats = mixed[:, block * 192 : block * 192 + 192]
            parts = []
            for z in range(8):
                w = w_ref[xh, y, z]
                tail = w[48:]
                tail = jnp.concatenate([tail[:, :64], tail[:, 64:]], 0)
                parts.append(jnp.concatenate([w[:48], tail], 1))
            wt = jnp.concatenate(parts, 0)
            term = lax.dot_general(feats, wt, NT, preferred_element_type=F32)
            total = term if total is None else total + term
    out = total.astype(BF)
    keep_ref[...] = out[:128]
    send_ref[...] = out[128:]


def assemble_kernel(at_ref, keep_ref, core_ref, chip_ref, o_ref):
    xl, core = at_ref[0], at_ref[1]
    mine, other = keep_ref[:64, :].astype(F32), core_ref[:64, :].astype(F32)
    far_mine, far_other = chip_ref[:64, :].astype(F32), chip_ref[64:, :].astype(F32)
    here0, here1 = jnp.where(core == 0, mine, other), jnp.where(core == 0, other, mine)
    far0, far1 = jnp.where(core == 0, far_mine, far_other), jnp.where(core == 0, far_other, far_mine)
    a0, a1 = jnp.where(xl == 0, here0, far0), jnp.where(xl == 0, here1, far1)
    b0, b1 = jnp.where(xl == 0, far0, here0), jnp.where(xl == 0, far1, here1)
    pieces = []
    for n in range(8):
        c = slice(n * 48, n * 48 + 48)
        pieces += [a0[:, c], a1[:, c], b0[:, c], b1[:, c]]
    o_ref[...] = jnp.concatenate(pieces, 1).astype(BF)


def call(kernel, outs, n_in, smem=(), limit=48):
    return pl.pallas_call(
        kernel,
        out_shape=outs,
        in_specs=[SM if k in smem else VM for k in range(n_in)],
        out_specs=VM if isinstance(outs, jax.ShapeDtypeStruct) else tuple(VM for _ in outs),
        compiler_params=pltpu.CompilerParams(vmem_limit_bytes=limit * 1024 * 1024),
    )


def shards(queries, key_tokens, values, position_bias, out_weight):
    width = queries.shape[3]
    rows, cols = ("z", "xl", "core"), ("xh", "y")
    nr, nc = lax.axis_size(rows), lax.axis_size(cols)
    r, c = lax.axis_index(rows), lax.axis_index(cols)

    down = [(n, n + 1) for n in range(nr - 1)]
    up = [(n + 1, n) for n in range(nr - 1)]
    right = [(n, n + 1) for n in range(nc - 1)]
    left = [(n + 1, n) for n in range(nc - 1)]
    k, v, q = (a.reshape(64, width) for a in (key_tokens, values, queries))
    wt = out_weight.T
    packed = jnp.concatenate([wt[:, :128], jnp.concatenate([wt[:24, 128:], wt[24:, 128:]], 1)], 0)
    along_z = lax.all_to_all(jnp.broadcast_to(packed[None], (8, 72, 128)), "z", 0, 0, tiled=True)

    top = lax.ppermute(jnp.concatenate([k[16:], v[16:]], 0), rows, down)
    bot = lax.ppermute(jnp.concatenate([k[:48], v[:48]], 0), rows, up)
    side = jax.ShapeDtypeStruct((64, width), BF)
    to_left, to_right = call(pack_kernel, (side, side), 5)(jnp.asarray(col_pick(), BF), k, v, top, bot)
    from_left = lax.ppermute(to_right, cols, right)
    from_right = lax.ppermute(to_left, cols, left)

    from_left, from_right, along_z = lax.optimization_barrier((from_left, from_right, along_z))
    plane = lax.all_to_all(
        jnp.broadcast_to(along_z[None], (8, 8, 72, 128)), ("xh", "y"), 0, 0, tiled=True
    )
    weights = plane.reshape(2, 4, 8, 72, 128)

    place = jnp.stack([r * 4, c * 16, nr * 4, nc * 16]).astype(jnp.int32)
    bias = jnp.pad(position_bias, ((0, 0), (0, 128 - 49)), constant_values=-jnp.inf)
    mixed = call(attention_kernel, side, 9, smem=(0,))(
        place, q, k, v, top, bot, from_left, from_right, bias
    )
    swap = [(0, 1), (1, 0)]
    next_mixed = lax.ppermute(mixed, "xl", swap)
    core_mixed = lax.ppermute(mixed, "core", swap)
    both_mixed = lax.ppermute(next_mixed, "core", swap)
    part = jax.ShapeDtypeStruct((128, width // 4), BF)
    keep, send = call(project_kernel, (part, part), 5)(mixed, next_mixed, core_mixed, both_mixed, weights)
    by_core = lax.ppermute(send, "core", swap)
    by_chip = lax.ppermute(jnp.concatenate([keep[64:], by_core[64:]], 0), "xl", swap)
    at = jnp.stack([lax.axis_index("xl"), lax.axis_index("core")]).astype(jnp.int32)
    out = call(assemble_kernel, side, 4, smem=(0,))(at, keep, by_core, by_chip)
    return out.reshape(queries.shape)


def solution(mesh):
    fine = Mesh(mesh.devices.reshape(8, 2, 2, 2, 4), ("z", "xl", "core", "xh", "y"))
    rows, cols = ("z", "xl", "core"), ("xh", "y")
    tokens = P(None, rows, cols, None)
    return jax.shard_map(
        shards,
        mesh=fine,
        in_specs=(tokens, tokens, tokens, P(), P(cols, rows)),
        out_specs=tokens,
        check_vma=False,
    )
```

```python
import jax
import jax.numpy as jnp
import numpy as np
from jax import lax
from jax.experimental import pallas as pl
from jax.experimental.pallas import tpu as pltpu
from jax.sharding import Mesh, PartitionSpec as P

VM = pl.BlockSpec(memory_space=pltpu.VMEM)
SM = pl.BlockSpec(memory_space=pltpu.SMEM)
BF = jnp.bfloat16
F32 = jnp.float32
NT = (((1,), (1,)), ((), ()))


def col_pick():
    pick = np.zeros((64, 160), np.float32)
    for side, first in ((0, 0), (1, 13)):
        for r in range(10):
            for j in range(3):
                x = first + j
                if r < 3:
                    source = 64 + r * 16 + x
                elif r < 7:
                    source = (r - 3) * 16 + x
                else:
                    source = 112 + (r - 7) * 16 + x
                pick[side * 32 + r * 3 + j, source] = 1.0
    return pick


def pack_kernel(pick_ref, k_ref, v_ref, top_ref, bot_ref, left_ref, right_ref):
    pick = pick_ref[...]
    for n, own in ((0, k_ref), (1, v_ref)):
        tokens = jnp.concatenate(
            [own[...], top_ref[n * 48 : n * 48 + 48, :], bot_ref[n * 48 : n * 48 + 48, :]], 0
        )
        got = jnp.dot(pick, tokens, preferred_element_type=F32).astype(BF)
        left_ref[n * 32 : n * 32 + 32, :] = got[:32]
        right_ref[n * 32 : n * 32 + 32, :] = got[32:]


def attention_kernel(
    place_ref, q_ref, k_ref, v_ref, top_ref, bot_ref, left_ref, right_ref, bias_ref, o_ref
):
    heads = bias_ref.shape[0]
    shape = (64, 256)
    i = lax.broadcasted_iota(jnp.int32, shape, 0)
    j = lax.broadcasted_iota(jnp.int32, shape, 1)
    y, x = i >> 4, i & 15
    side = j & 31
    side_row = ((side * 171) >> 9) - 3
    side_col = side - (side_row + 3) * 3
    ky = jnp.where(
        j < 64,
        j >> 4,
        jnp.where(j < 112, (j >> 4) - 7, jnp.where(j < 160, (j >> 4) - 3, side_row)),
    )
    kx = jnp.where(j < 160, j & 15, jnp.where(j < 192, side_col - 3, side_col + 16))
    dy, dx = ky - y + 3, kx - x + 3
    gy, gx = ky + place_ref[0], kx + place_ref[1]
    inside = (dy >= 0) & (dy < 7) & (dx >= 0) & (dx < 7)
    inside = inside & (gy >= 0) & (gy < place_ref[2]) & (gx >= 0) & (gx < place_ref[3])
    inside = inside & ((j < 160) | (side < 30)) & (j < 224)
    code = jnp.where(inside, dy * 7 + dx, 127)
    code_low, code_high = code[:, :128], code[:, 128:]
    low = lax.broadcasted_iota(jnp.int32, (64, 128), 1) < 64
    zeros = jnp.zeros((32, 128), BF)
    none = jnp.zeros((64, 128), BF)

    for pair in range(heads // 2):
        c = slice(pair * 128, pair * 128 + 128)
        q = q_ref[:, c]
        q2 = jnp.concatenate([jnp.where(low, q, none), jnp.where(low, none, q)], 0)
        keys = jnp.concatenate(
            [k_ref[:, c], top_ref[:48, c], bot_ref[:48, c], left_ref[:32, c], right_ref[:32, c], zeros], 0
        )
        vals = jnp.concatenate(
            [v_ref[:, c], top_ref[48:, c], bot_ref[48:, c], left_ref[32:, c], right_ref[32:, c], zeros], 0
        )
        s = lax.dot_general(q2, keys, NT, preferred_element_type=F32)
        bias = []
        for h in (2 * pair, 2 * pair + 1):
            row = jnp.broadcast_to(bias_ref[h : h + 1, :], (64, 128))
            bias.append(
                jnp.concatenate(
                    [
                        jnp.take_along_axis(row, code_low, axis=1, mode="promise_in_bounds"),
                        jnp.take_along_axis(row, code_high, axis=1, mode="promise_in_bounds"),
                    ],
                    1,
                )
            )
        s = s * 0.125 + jnp.concatenate(bias, 0)
        e = jnp.exp(s - jnp.max(s, 1, keepdims=True))
        p = (e * (1.0 / jnp.sum(e, 1, keepdims=True))).astype(BF)
        o = jnp.dot(p, vals, preferred_element_type=F32)
        o_ref[:, c] = jnp.where(low, o[:64], o[64:]).astype(BF)


def project_kernel(a_ref, b_ref, c_ref, d_ref, w_ref, keep_ref, chip_ref, core_ref, both_ref):
    mixed = jnp.concatenate([a_ref[...], b_ref[...], c_ref[...], d_ref[...]], 0)
    total = None
    for xh in range(2):
        for y in range(4):
            block = xh * 4 + y
            feats = mixed[:, block * 192 : block * 192 + 192]
            parts = []
            for z in range(8):
                w = w_ref[xh, y, z]
                tail = w[48:]
                tail = jnp.concatenate([tail[:, :64], tail[:, 64:]], 0)
                parts.append(jnp.concatenate([w[:48], tail], 1))
            wt = jnp.concatenate(parts, 0)
            term = lax.dot_general(feats, wt, NT, preferred_element_type=F32)
            total = term if total is None else total + term
    out = total.astype(BF)
    for n, ref in enumerate((keep_ref, chip_ref, core_ref, both_ref)):
        ref[...] = out[n * 64 : n * 64 + 64]


def assemble_kernel(at_ref, keep_ref, core_ref, chip_ref, both_ref, o_ref):
    xl, core = at_ref[0] == 0, at_ref[1] == 0
    mine, other, far, far_other = (ref[...].astype(F32) for ref in (keep_ref, core_ref, chip_ref, both_ref))
    here0, here1 = jnp.where(core, mine, other), jnp.where(core, other, mine)
    far0, far1 = jnp.where(core, far, far_other), jnp.where(core, far_other, far)
    quarters = (
        jnp.where(xl, here0, far0),
        jnp.where(xl, here1, far1),
        jnp.where(xl, far0, here0),
        jnp.where(xl, far1, here1),
    )
    pieces = [part[:, n * 48 : n * 48 + 48] for n in range(8) for part in quarters]
    o_ref[...] = jnp.concatenate(pieces, 1).astype(BF)


def call(kernel, outs, n_in, smem=(), limit=48):
    return pl.pallas_call(
        kernel,
        out_shape=outs,
        in_specs=[SM if k in smem else VM for k in range(n_in)],
        out_specs=VM if isinstance(outs, jax.ShapeDtypeStruct) else tuple(VM for _ in outs),
        compiler_params=pltpu.CompilerParams(vmem_limit_bytes=limit * 1024 * 1024),
    )


def shards(queries, key_tokens, values, position_bias, out_weight):
    width = queries.shape[3]
    rows, cols = ("z", "xl", "core"), ("xh", "y")
    nr, nc = lax.axis_size(rows), lax.axis_size(cols)
    r, c = lax.axis_index(rows), lax.axis_index(cols)

    down = [(n, (n + 1) % nr) for n in range(nr)]
    up = [(n, (n - 1) % nr) for n in range(nr)]
    right = [(n, (n + 1) % nc) for n in range(nc)]
    left = [(n, (n - 1) % nc) for n in range(nc)]
    k, v, q = (a.reshape(64, width) for a in (key_tokens, values, queries))
    wt = out_weight.T
    packed = jnp.concatenate([wt[:, :128], jnp.concatenate([wt[:24, 128:], wt[24:, 128:]], 1)], 0)
    along_z = lax.all_to_all(jnp.broadcast_to(packed[None], (8, 72, 128)), "z", 0, 0, tiled=True)

    both = jnp.stack([k, v], 0)
    top = lax.ppermute(both[:, 16:], rows, down).reshape(96, width)
    bot = lax.ppermute(both[:, :48], rows, up).reshape(96, width)
    side = jax.ShapeDtypeStruct((64, width), BF)
    to_left, to_right = call(pack_kernel, (side, side), 5)(jnp.asarray(col_pick(), BF), k, v, top, bot)
    from_left = lax.ppermute(to_right, cols, right)
    from_right = lax.ppermute(to_left, cols, left)

    from_left, from_right, along_z = lax.optimization_barrier((from_left, from_right, along_z))
    plane = lax.all_to_all(
        jnp.broadcast_to(along_z[None], (8, 8, 72, 128)), ("xh", "y"), 0, 0, tiled=True
    )
    weights = plane.reshape(2, 4, 8, 72, 128)

    place = jnp.stack([r * 4, c * 16, nr * 4, nc * 16]).astype(jnp.int32)
    bias = jnp.pad(position_bias, ((0, 0), (0, 128 - 49)), constant_values=-jnp.inf)
    mixed = call(attention_kernel, side, 9, smem=(0,))(
        place, q, k, v, top, bot, from_left, from_right, bias
    )
    swap = [(0, 1), (1, 0)]
    next_mixed = lax.ppermute(mixed, "xl", swap)
    core_mixed = lax.ppermute(mixed, "core", swap)
    both_mixed = lax.ppermute(next_mixed, "core", swap)
    part = jax.ShapeDtypeStruct((64, width // 4), BF)
    keep, to_chip, to_core, to_both = call(project_kernel, (part,) * 4, 5)(
        mixed, next_mixed, core_mixed, both_mixed, weights
    )
    by_both = lax.ppermute(to_both, ("xl", "core"), [(n, 3 - n) for n in range(4)])
    by_chip = lax.ppermute(to_chip, "xl", swap)
    by_core = lax.ppermute(to_core, "core", swap)
    at = jnp.stack([lax.axis_index("xl"), lax.axis_index("core")]).astype(jnp.int32)
    out = call(assemble_kernel, side, 5, smem=(0,))(at, keep, by_core, by_chip, by_both)
    return out.reshape(queries.shape)


def solution(mesh):
    fine = Mesh(mesh.devices.reshape(8, 2, 2, 2, 4), ("z", "xl", "core", "xh", "y"))
    rows, cols = ("z", "xl", "core"), ("xh", "y")
    tokens = P(None, rows, cols, None)
    return jax.shard_map(
        shards,
        mesh=fine,
        in_specs=(tokens, tokens, tokens, P(), P(cols, rows)),
        out_specs=tokens,
        check_vma=False,
    )
```

```python
import jax
import jax.numpy as jnp
import numpy as np
from jax import lax
from jax.experimental import pallas as pl
from jax.experimental.pallas import tpu as pltpu
from jax.sharding import Mesh, PartitionSpec as P

VM = pl.BlockSpec(memory_space=pltpu.VMEM)
SM = pl.BlockSpec(memory_space=pltpu.SMEM)
BF = jnp.bfloat16
F32 = jnp.float32
NT = (((1,), (1,)), ((), ()))


def col_pick():
    pick = np.zeros((64, 160), np.float32)
    for side, first in ((0, 0), (1, 13)):
        for r in range(10):
            for j in range(3):
                x = first + j
                if r < 3:
                    source = 64 + r * 16 + x
                elif r < 7:
                    source = (r - 3) * 16 + x
                else:
                    source = 112 + (r - 7) * 16 + x
                pick[side * 32 + r * 3 + j, source] = 1.0
    return pick


def weight_kernel(wt_ref, out_ref):
    w = wt_ref[...]
    packed = jnp.concatenate([w[:, :128], jnp.concatenate([w[:24, 128:], w[24:, 128:]], 1)], 0)
    for n in range(out_ref.shape[0]):
        out_ref[n] = packed


def pack_kernel(pick_ref, k_ref, v_ref, top_ref, bot_ref, left_ref, right_ref):
    pick = pick_ref[...]
    for n, own in ((0, k_ref), (1, v_ref)):
        tokens = jnp.concatenate(
            [own[...], top_ref[n * 48 : n * 48 + 48, :], bot_ref[n * 48 : n * 48 + 48, :]], 0
        )
        got = jnp.dot(pick, tokens, preferred_element_type=F32).astype(BF)
        left_ref[n * 32 : n * 32 + 32, :] = got[:32]
        right_ref[n * 32 : n * 32 + 32, :] = got[32:]


def attention_kernel(
    place_ref, q_ref, k_ref, v_ref, top_ref, bot_ref, left_ref, right_ref, bias_ref, o_ref
):
    heads = bias_ref.shape[0]
    shape = (64, 256)
    i = lax.broadcasted_iota(jnp.int32, shape, 0)
    j = lax.broadcasted_iota(jnp.int32, shape, 1)
    y, x = i >> 4, i & 15
    side = j & 31
    side_row = ((side * 171) >> 9) - 3
    side_col = side - (side_row + 3) * 3
    ky = jnp.where(
        j < 64,
        j >> 4,
        jnp.where(j < 112, (j >> 4) - 7, jnp.where(j < 160, (j >> 4) - 3, side_row)),
    )
    kx = jnp.where(j < 160, j & 15, jnp.where(j < 192, side_col - 3, side_col + 16))
    dy, dx = ky - y + 3, kx - x + 3
    gy, gx = ky + place_ref[0], kx + place_ref[1]
    inside = (dy >= 0) & (dy < 7) & (dx >= 0) & (dx < 7)
    inside = inside & (gy >= 0) & (gy < place_ref[2]) & (gx >= 0) & (gx < place_ref[3])
    inside = inside & ((j < 160) | (side < 30)) & (j < 224)
    code = jnp.where(inside, dy * 7 + dx, 127)
    code_low, code_high = code[:, :128], code[:, 128:]
    low = lax.broadcasted_iota(jnp.int32, (64, 128), 1) < 64
    zeros = jnp.zeros((32, 128), BF)
    none = jnp.zeros((64, 128), BF)

    for pair in range(heads // 2):
        c = slice(pair * 128, pair * 128 + 128)
        q = q_ref[:, c]
        q2 = jnp.concatenate([jnp.where(low, q, none), jnp.where(low, none, q)], 0)
        keys = jnp.concatenate(
            [k_ref[:, c], top_ref[:48, c], bot_ref[:48, c], left_ref[:32, c], right_ref[:32, c], zeros], 0
        )
        vals = jnp.concatenate(
            [v_ref[:, c], top_ref[48:, c], bot_ref[48:, c], left_ref[32:, c], right_ref[32:, c], zeros], 0
        )
        s = lax.dot_general(q2, keys, NT, preferred_element_type=F32)
        bias = []
        for h in (2 * pair, 2 * pair + 1):
            row = jnp.broadcast_to(bias_ref[h : h + 1, :], (64, 128))
            bias.append(
                jnp.concatenate(
                    [
                        jnp.take_along_axis(row, code_low, axis=1, mode="promise_in_bounds"),
                        jnp.take_along_axis(row, code_high, axis=1, mode="promise_in_bounds"),
                    ],
                    1,
                )
            )
        s = s * 0.125 + jnp.concatenate(bias, 0)
        e = jnp.exp(s - jnp.max(s, 1, keepdims=True))
        p = (e * (1.0 / jnp.sum(e, 1, keepdims=True))).astype(BF)
        o = jnp.dot(p, vals, preferred_element_type=F32)
        o_ref[:, c] = jnp.where(low, o[:64], o[64:]).astype(BF)


def unpack_kernel(w0_ref, w1_ref, w3_ref, w2_ref, out_ref):
    for xh in range(2):
        for k, w_ref in enumerate((w0_ref, w1_ref, w2_ref, w3_ref)):
            for z in range(8):
                w = w_ref[xh, z]
                tail = w[48:]
                tail = jnp.concatenate([tail[:, :64], tail[:, 64:]], 0)
                out_ref[xh * 4 + k, z * 48 : z * 48 + 48, :] = jnp.concatenate([w[:48], tail], 1)


def project_kernel(y_ref, a_ref, b_ref, c_ref, d_ref, w_ref, keep_ref, chip_ref, core_ref, both_ref):
    mixed = jnp.concatenate([a_ref[...], b_ref[...], c_ref[...], d_ref[...]], 0)
    odd, upper = (y_ref[0] & 1) == 1, y_ref[0] >= 2
    total = None
    for xh in range(2):
        f = [mixed[:, xh * 768 + n * 192 : xh * 768 + n * 192 + 192] for n in range(4)]
        f = [jnp.where(odd, f[n ^ 1], f[n]) for n in range(4)]
        f = [jnp.where(upper, f[n ^ 2], f[n]) for n in range(4)]
        for k in range(4):
            term = lax.dot_general(f[k], w_ref[xh * 4 + k], NT, preferred_element_type=F32)
            total = term if total is None else total + term
    out = total.astype(BF)
    for n, ref in enumerate((keep_ref, chip_ref, core_ref, both_ref)):
        ref[...] = out[n * 64 : n * 64 + 64]


def assemble_kernel(at_ref, keep_ref, core_ref, chip_ref, both_ref, o_ref):
    parts = (keep_ref, core_ref, chip_ref, both_ref)
    for me in range(4):

        @pl.when(at_ref[0] * 2 + at_ref[1] == me)
        def _():
            quarters = [parts[me ^ q][...] for q in range(4)]
            pieces = [part[:, n * 48 : n * 48 + 48] for n in range(8) for part in quarters]
            o_ref[...] = jnp.concatenate(pieces, 1)


def call(kernel, outs, n_in, smem=(), limit=48, flops=0):
    cost = pl.CostEstimate(flops=flops, bytes_accessed=4 * 1024 * 1024, transcendentals=0) if flops else None
    return pl.pallas_call(
        kernel,
        out_shape=outs,
        in_specs=[SM if k in smem else VM for k in range(n_in)],
        out_specs=VM if isinstance(outs, jax.ShapeDtypeStruct) else tuple(VM for _ in outs),
        cost_estimate=cost,
        compiler_params=pltpu.CompilerParams(vmem_limit_bytes=limit * 1024 * 1024),
    )


def shards(queries, key_tokens, values, position_bias, out_weight):
    width = queries.shape[3]
    rows, cols = ("z", "xl", "core"), ("xh", "y")
    nr, nc = lax.axis_size(rows), lax.axis_size(cols)
    r, c = lax.axis_index(rows), lax.axis_index(cols)

    down = [(n, (n + 1) % nr) for n in range(nr)]
    up = [(n, (n - 1) % nr) for n in range(nr)]
    right = [(n, (n + 1) % nc) for n in range(nc)]
    left = [(n, (n - 1) % nc) for n in range(nc)]
    k, v, q = (a.reshape(64, width) for a in (key_tokens, values, queries))
    packed = call(weight_kernel, jax.ShapeDtypeStruct((16, 72, 128), BF), 1)(out_weight.T)
    along_zx = lax.all_to_all(packed, ("xh", "z"), 0, 0, tiled=True)

    both = jnp.stack([k, v], 0)
    top = lax.ppermute(both[:, 16:], rows, down).reshape(96, width)
    bot = lax.ppermute(both[:, :48], rows, up).reshape(96, width)
    side = jax.ShapeDtypeStruct((64, width), BF)
    to_left, to_right = call(pack_kernel, (side, side), 5, flops=50000000000)(jnp.asarray(col_pick(), BF), k, v, top, bot)
    from_left = lax.ppermute(to_right, cols, right)
    from_right = lax.ppermute(to_left, cols, left)

    near = along_zx.reshape(2, 8, 72, 128)
    stages = [near] + [lax.ppermute(near, "y", [(n, n ^ k) for n in range(4)]) for k in (1, 3, 2)]

    place = jnp.stack([r * 4, c * 16, nr * 4, nc * 16]).astype(jnp.int32)
    bias = jnp.pad(position_bias, ((0, 0), (0, 128 - 49)), constant_values=-jnp.inf)
    mixed = call(attention_kernel, side, 9, smem=(0,), flops=50000000000)(
        place, q, k, v, top, bot, from_left, from_right, bias
    )
    swap = [(0, 1), (1, 0)]
    next_mixed = lax.ppermute(mixed, "xl", swap)
    core_mixed = lax.ppermute(mixed, "core", swap)
    both_mixed = lax.ppermute(next_mixed, "core", swap)
    weights = call(unpack_kernel, jax.ShapeDtypeStruct((8, 384, 192), BF), 4, flops=100000000000)(*stages)
    part = jax.ShapeDtypeStruct((64, width // 4), BF)
    y = lax.axis_index("y").astype(jnp.int32).reshape(1)
    keep, to_chip, to_core, to_both = call(project_kernel, (part,) * 4, 6, smem=(0,))(
        y, mixed, next_mixed, core_mixed, both_mixed, weights
    )
    by_both = lax.ppermute(to_both, ("xl", "core"), [(n, 3 - n) for n in range(4)])
    by_chip = lax.ppermute(to_chip, "xl", swap)
    by_core = lax.ppermute(to_core, "core", swap)
    at = jnp.stack([lax.axis_index("xl"), lax.axis_index("core")]).astype(jnp.int32)
    out = call(assemble_kernel, side, 5, smem=(0,))(at, keep, by_core, by_chip, by_both)
    return out.reshape(queries.shape)


def solution(mesh):
    fine = Mesh(mesh.devices.reshape(8, 2, 2, 2, 4), ("z", "xl", "core", "xh", "y"))
    rows, cols = ("z", "xl", "core"), ("xh", "y")
    tokens = P(None, rows, cols, None)
    return jax.shard_map(
        shards,
        mesh=fine,
        in_specs=(tokens, tokens, tokens, P(), P(cols, rows)),
        out_specs=tokens,
        check_vma=False,
    )
```

```python
import jax
import jax.numpy as jnp
from jax import lax
from jax.experimental import pallas as pl
from jax.experimental.pallas import tpu as pltpu
from jax.sharding import Mesh, PartitionSpec as P

VM = pl.BlockSpec(memory_space=pltpu.VMEM)
SM = pl.BlockSpec(memory_space=pltpu.SMEM)
BF = jnp.bfloat16
F32 = jnp.float32
NT = (((1,), (1,)), ((), ()))


def weight_kernel(wt_ref, out_ref):
    w = wt_ref[...]
    packed = jnp.concatenate([w[:, :128], jnp.concatenate([w[:24, 128:], w[24:, 128:]], 1)], 0)
    for n in range(out_ref.shape[0]):
        out_ref[n] = packed


def pack_kernel(up_ref, down_ref, top_ref, bot_ref, left_ref, right_ref):
    i = lax.broadcasted_iota(jnp.int32, (64, 160), 0)
    source = lax.broadcasted_iota(jnp.int32, (64, 160), 1)
    t = i & 31
    r = (t * 171) >> 9
    x = t - r * 3 + (i >> 5) * 13
    start = jnp.where(r < 3, r * 16 + 64, jnp.where(r < 7, r * 16 - 48, r * 16))
    pick = jnp.where((source == start + x) & (t < 30), 1.0, 0.0).astype(BF)
    for n in range(2):
        tokens = jnp.concatenate(
            [up_ref[n], down_ref[n, 32:, :], top_ref[n * 48 : n * 48 + 48, :], bot_ref[n * 48 : n * 48 + 48, :]], 0
        )
        got = jnp.dot(pick, tokens, preferred_element_type=F32).astype(BF)
        left_ref[n * 32 : n * 32 + 32, :] = got[:32]
        right_ref[n * 32 : n * 32 + 32, :] = got[32:]


def attention_kernel(
    place_ref, q_ref, k_ref, v_ref, top_ref, bot_ref, left_ref, right_ref, bias_ref, o_ref
):
    heads = bias_ref.shape[0]
    shape = (64, 256)
    i = lax.broadcasted_iota(jnp.int32, shape, 0)
    j = lax.broadcasted_iota(jnp.int32, shape, 1)
    y, x = i >> 4, i & 15
    side = j & 31
    side_row = ((side * 171) >> 9) - 3
    side_col = side - (side_row + 3) * 3
    ky = jnp.where(
        j < 64,
        j >> 4,
        jnp.where(j < 112, (j >> 4) - 7, jnp.where(j < 160, (j >> 4) - 3, side_row)),
    )
    kx = jnp.where(j < 160, j & 15, jnp.where(j < 192, side_col - 3, side_col + 16))
    dy, dx = ky - y + 3, kx - x + 3
    gy, gx = ky + place_ref[0], kx + place_ref[1]
    inside = (dy >= 0) & (dy < 7) & (dx >= 0) & (dx < 7)
    inside = inside & (gy >= 0) & (gy < place_ref[2]) & (gx >= 0) & (gx < place_ref[3])
    inside = inside & ((j < 160) | (side < 30)) & (j < 224)
    code = jnp.where(inside, dy * 7 + dx, 127)
    code_low, code_high = code[:, :128], code[:, 128:]
    low = lax.broadcasted_iota(jnp.int32, (64, 128), 1) < 64
    zeros = jnp.zeros((32, 128), BF)
    none = jnp.zeros((64, 128), BF)

    for pair in range(heads // 2):
        c = slice(pair * 128, pair * 128 + 128)
        q = q_ref[:, c]
        q2 = jnp.concatenate([jnp.where(low, q, none), jnp.where(low, none, q)], 0)
        keys = jnp.concatenate(
            [k_ref[:, c], top_ref[:48, c], bot_ref[:48, c], left_ref[:32, c], right_ref[:32, c], zeros], 0
        )
        vals = jnp.concatenate(
            [v_ref[:, c], top_ref[48:, c], bot_ref[48:, c], left_ref[32:, c], right_ref[32:, c], zeros], 0
        )
        s = lax.dot_general(q2, keys, NT, preferred_element_type=F32)
        bias = []
        for h in (2 * pair, 2 * pair + 1):
            row = jnp.broadcast_to(bias_ref[h : h + 1, :], (64, 128))
            bias.append(
                jnp.concatenate(
                    [
                        jnp.take_along_axis(row, code_low, axis=1, mode="promise_in_bounds"),
                        jnp.take_along_axis(row, code_high, axis=1, mode="promise_in_bounds"),
                    ],
                    1,
                )
            )
        s = s * 0.125 + jnp.concatenate(bias, 0)
        e = jnp.exp(s - jnp.max(s, 1, keepdims=True))
        p = (e * (1.0 / jnp.sum(e, 1, keepdims=True))).astype(BF)
        o = jnp.dot(p, vals, preferred_element_type=F32)
        o_ref[:, c] = jnp.where(low, o[:64], o[64:]).astype(BF)


def unpack_kernel(w0_ref, w1_ref, w3_ref, w2_ref, out_ref):
    for xh in range(2):
        for k, w_ref in enumerate((w0_ref, w1_ref, w2_ref, w3_ref)):
            for z in range(8):
                w = w_ref[xh, z]
                tail = w[48:]
                tail = jnp.concatenate([tail[:, :64], tail[:, 64:]], 0)
                out_ref[xh * 4 + k, z * 48 : z * 48 + 48, :] = jnp.concatenate([w[:48], tail], 1)


def project_kernel(y_ref, a_ref, b_ref, c_ref, d_ref, w_ref, keep_ref, chip_ref, core_ref, both_ref):
    mixed = jnp.concatenate([a_ref[...], b_ref[...], c_ref[...], d_ref[...]], 0)
    odd, upper = (y_ref[0] & 1) == 1, y_ref[0] >= 2
    total = None
    for xh in range(2):
        f = [mixed[:, xh * 768 + n * 192 : xh * 768 + n * 192 + 192] for n in range(4)]
        f = [jnp.where(odd, f[n ^ 1], f[n]) for n in range(4)]
        f = [jnp.where(upper, f[n ^ 2], f[n]) for n in range(4)]
        for k in range(4):
            term = lax.dot_general(f[k], w_ref[xh * 4 + k], NT, preferred_element_type=F32)
            total = term if total is None else total + term
    out = total.astype(BF)
    for n, ref in enumerate((keep_ref, chip_ref, core_ref, both_ref)):
        ref[...] = out[n * 64 : n * 64 + 64]


def assemble_kernel(at_ref, keep_ref, core_ref, chip_ref, both_ref, o_ref):
    parts = (keep_ref, core_ref, chip_ref, both_ref)
    for me in range(4):

        @pl.when(at_ref[0] * 2 + at_ref[1] == me)
        def _():
            quarters = [parts[me ^ q][...] for q in range(4)]
            pieces = [part[:, n * 48 : n * 48 + 48] for n in range(8) for part in quarters]
            o_ref[...] = jnp.concatenate(pieces, 1)


def call(kernel, outs, n_in, smem=(), limit=48, flops=0):
    cost = pl.CostEstimate(flops=flops, bytes_accessed=4 * 1024 * 1024, transcendentals=0) if flops else None
    return pl.pallas_call(
        kernel,
        out_shape=outs,
        in_specs=[SM if k in smem else VM for k in range(n_in)],
        out_specs=VM if isinstance(outs, jax.ShapeDtypeStruct) else tuple(VM for _ in outs),
        cost_estimate=cost,
        compiler_params=pltpu.CompilerParams(vmem_limit_bytes=limit * 1024 * 1024),
    )


def shards(queries, key_tokens, values, position_bias, out_weight):
    width = queries.shape[3]
    rows, cols = ("z", "xl", "core"), ("xh", "y")
    nr, nc = lax.axis_size(rows), lax.axis_size(cols)
    r, c = lax.axis_index(rows), lax.axis_index(cols)

    down = [(n, (n + 1) % nr) for n in range(nr)]
    up = [(n, (n - 1) % nr) for n in range(nr)]
    right = [(n, (n + 1) % nc) for n in range(nc)]
    left = [(n, (n - 1) % nc) for n in range(nc)]
    k, v, q = (a.reshape(64, width) for a in (key_tokens, values, queries))
    packed = call(weight_kernel, jax.ShapeDtypeStruct((16, 72, 128), BF), 1)(out_weight.T)
    along_zx = lax.all_to_all(packed, ("xh", "z"), 0, 0, tiled=True)

    both = jnp.stack([k, v], 0)
    to_down, to_up = both[:, 16:], both[:, :48]
    top = lax.ppermute(to_down, rows, down).reshape(96, width)
    bot = lax.ppermute(to_up, rows, up).reshape(96, width)
    side = jax.ShapeDtypeStruct((64, width), BF)
    to_left, to_right = call(pack_kernel, (side, side), 4, flops=50000000000)(to_up, to_down, top, bot)
    from_left = lax.ppermute(to_right, cols, right)
    from_right = lax.ppermute(to_left, cols, left)

    near = along_zx.reshape(2, 8, 72, 128)
    stages = [near] + [lax.ppermute(near, "y", [(n, n ^ k) for n in range(4)]) for k in (1, 3, 2)]

    place = jnp.stack([r * 4, c * 16, nr * 4, nc * 16]).astype(jnp.int32)
    bias = jnp.pad(position_bias, ((0, 0), (0, 128 - 49)), constant_values=-jnp.inf)
    mixed = call(attention_kernel, side, 9, smem=(0,), flops=50000000000)(
        place, q, k, v, top, bot, from_left, from_right, bias
    )
    swap = [(0, 1), (1, 0)]
    next_mixed = lax.ppermute(mixed, "xl", swap)
    core_mixed = lax.ppermute(mixed, "core", swap)
    both_mixed = lax.ppermute(next_mixed, "core", swap)
    weights = call(unpack_kernel, jax.ShapeDtypeStruct((8, 384, 192), BF), 4, flops=100000000000)(*stages)
    part = jax.ShapeDtypeStruct((64, width // 4), BF)
    y = lax.axis_index("y").astype(jnp.int32).reshape(1)
    keep, to_chip, to_core, to_both = call(project_kernel, (part,) * 4, 6, smem=(0,))(
        y, mixed, next_mixed, core_mixed, both_mixed, weights
    )
    by_both = lax.ppermute(to_both, ("xl", "core"), [(n, 3 - n) for n in range(4)])
    by_chip = lax.ppermute(to_chip, "xl", swap)
    by_core = lax.ppermute(to_core, "core", swap)
    at = jnp.stack([lax.axis_index("xl"), lax.axis_index("core")]).astype(jnp.int32)
    out = call(assemble_kernel, side, 5, smem=(0,))(at, keep, by_core, by_chip, by_both)
    return out.reshape(queries.shape)


def solution(mesh):
    fine = Mesh(mesh.devices.reshape(8, 2, 2, 2, 4), ("z", "xl", "core", "xh", "y"))
    rows, cols = ("z", "xl", "core"), ("xh", "y")
    tokens = P(None, rows, cols, None)
    return jax.shard_map(
        shards,
        mesh=fine,
        in_specs=(tokens, tokens, tokens, P(), P(cols, rows)),
        out_specs=tokens,
        check_vma=False,
    )
```

```python
import jax
import jax.numpy as jnp
from jax import lax
from jax.experimental import pallas as pl
from jax.experimental.pallas import tpu as pltpu
from jax.sharding import Mesh, PartitionSpec as P

VM = pl.BlockSpec(memory_space=pltpu.VMEM)
SM = pl.BlockSpec(memory_space=pltpu.SMEM)
BF = jnp.bfloat16
F32 = jnp.float32
NT = (((1,), (1,)), ((), ()))


def weight_kernel(wt_ref, out_ref):
    w = wt_ref[...]
    packed = jnp.concatenate([w[:, :128], jnp.concatenate([w[:24, 128:], w[24:, 128:]], 1)], 0)
    for n in range(out_ref.shape[0]):
        out_ref[n] = packed


def pack_kernel(up_ref, down_ref, top_ref, bot_ref, left_ref, right_ref):
    i = lax.broadcasted_iota(jnp.int32, (64, 160), 0)
    source = lax.broadcasted_iota(jnp.int32, (64, 160), 1)
    t = i & 31
    r = (t * 171) >> 9
    x = t - r * 3 + (i >> 5) * 13
    start = jnp.where(r < 3, r * 16 + 64, jnp.where(r < 7, r * 16 - 48, r * 16))
    pick = jnp.where((source == start + x) & (t < 30), 1.0, 0.0).astype(BF)
    for n in range(2):
        tokens = jnp.concatenate(
            [up_ref[n], down_ref[n, 32:, :], top_ref[n * 48 : n * 48 + 48, :], bot_ref[n * 48 : n * 48 + 48, :]], 0
        )
        got = jnp.dot(pick, tokens, preferred_element_type=F32).astype(BF)
        left_ref[n * 32 : n * 32 + 32, :] = got[:32]
        right_ref[n * 32 : n * 32 + 32, :] = got[32:]


def attention_kernel(
    place_ref, q_ref, k_ref, v_ref, top_ref, bot_ref, left_ref, right_ref, bias_ref, o_ref
):
    heads = bias_ref.shape[0]
    shape = (64, 256)
    i = lax.broadcasted_iota(jnp.int32, shape, 0)
    j = lax.broadcasted_iota(jnp.int32, shape, 1)
    y, x = i >> 4, i & 15
    side = j & 31
    side_row = ((side * 171) >> 9) - 3
    side_col = side - (side_row + 3) * 3
    ky = jnp.where(
        j < 64,
        j >> 4,
        jnp.where(j < 112, (j >> 4) - 7, jnp.where(j < 160, (j >> 4) - 3, side_row)),
    )
    kx = jnp.where(j < 160, j & 15, jnp.where(j < 192, side_col - 3, side_col + 16))
    dy, dx = ky - y + 3, kx - x + 3
    gy, gx = ky + place_ref[0], kx + place_ref[1]
    inside = (dy >= 0) & (dy < 7) & (dx >= 0) & (dx < 7)
    inside = inside & (gy >= 0) & (gy < place_ref[2]) & (gx >= 0) & (gx < place_ref[3])
    inside = inside & ((j < 160) | (side < 30)) & (j < 224)
    code = jnp.where(inside, dy * 7 + dx, 127)
    code_low, code_high = code[:, :128], code[:, 128:]
    low = lax.broadcasted_iota(jnp.int32, (64, 128), 1) < 64
    zeros = jnp.zeros((32, 128), BF)
    none = jnp.zeros((64, 128), BF)

    for pair in range(heads // 2):
        c = slice(pair * 128, pair * 128 + 128)
        q = q_ref[:, c]
        q2 = jnp.concatenate([jnp.where(low, q, none), jnp.where(low, none, q)], 0)
        keys = jnp.concatenate(
            [k_ref[:, c], top_ref[:48, c], bot_ref[:48, c], left_ref[:32, c], right_ref[:32, c], zeros], 0
        )
        vals = jnp.concatenate(
            [v_ref[:, c], top_ref[48:, c], bot_ref[48:, c], left_ref[32:, c], right_ref[32:, c], zeros], 0
        )
        s = lax.dot_general(q2, keys, NT, preferred_element_type=F32)
        bias = []
        for h in (2 * pair, 2 * pair + 1):
            row = jnp.broadcast_to(bias_ref[h : h + 1, :], (64, 128))
            bias.append(
                jnp.concatenate(
                    [
                        jnp.take_along_axis(row, code_low, axis=1, mode="promise_in_bounds"),
                        jnp.take_along_axis(row, code_high, axis=1, mode="promise_in_bounds"),
                    ],
                    1,
                )
            )
        s = s * 0.125 + jnp.concatenate(bias, 0)
        e = jnp.exp(s - jnp.max(s, 1, keepdims=True))
        p = (e * (1.0 / jnp.sum(e, 1, keepdims=True))).astype(BF)
        o = jnp.dot(p, vals, preferred_element_type=F32)
        o_ref[:, c] = jnp.where(low, o[:64], o[64:]).astype(BF)


def unpack_kernel(w0_ref, w1_ref, w3_ref, w2_ref, out_ref):
    for xh in range(2):
        for k, w_ref in enumerate((w0_ref, w1_ref, w2_ref, w3_ref)):
            for z in range(8):
                w = w_ref[xh, z]
                tail = w[48:]
                tail = jnp.concatenate([tail[:, :64], tail[:, 64:]], 0)
                out_ref[xh * 4 + k, z * 48 : z * 48 + 48, :] = jnp.concatenate([w[:48], tail], 1)


def project_kernel(y_ref, a_ref, b_ref, c_ref, d_ref, w_ref, keep_ref, chip_ref, core_ref, both_ref):
    mixed = jnp.concatenate([a_ref[...], b_ref[...], c_ref[...], d_ref[...]], 0)
    odd, upper = (y_ref[0] & 1) == 1, y_ref[0] >= 2
    total = None
    for xh in range(2):
        f = [mixed[:, xh * 768 + n * 192 : xh * 768 + n * 192 + 192] for n in range(4)]
        f = [jnp.where(odd, f[n ^ 1], f[n]) for n in range(4)]
        f = [jnp.where(upper, f[n ^ 2], f[n]) for n in range(4)]
        for k in range(4):
            term = lax.dot_general(f[k], w_ref[xh * 4 + k], NT, preferred_element_type=F32)
            total = term if total is None else total + term
    out = total.astype(BF)
    for n, ref in enumerate((keep_ref, chip_ref, core_ref, both_ref)):
        ref[...] = out[n * 64 : n * 64 + 64]


def assemble_kernel(at_ref, keep_ref, core_ref, chip_ref, both_ref, o_ref):
    parts = (keep_ref, core_ref, chip_ref, both_ref)
    for me in range(4):

        @pl.when(at_ref[0] * 2 + at_ref[1] == me)
        def _():
            quarters = [parts[me ^ q][...] for q in range(4)]
            pieces = [part[:, n * 48 : n * 48 + 48] for n in range(8) for part in quarters]
            o_ref[...] = jnp.concatenate(pieces, 1)


def call(kernel, outs, n_in, smem=(), limit=48, flops=0):
    cost = pl.CostEstimate(flops=flops, bytes_accessed=4 * 1024 * 1024, transcendentals=0) if flops else None
    return pl.pallas_call(
        kernel,
        out_shape=outs,
        in_specs=[SM if k in smem else VM for k in range(n_in)],
        out_specs=VM if isinstance(outs, jax.ShapeDtypeStruct) else tuple(VM for _ in outs),
        cost_estimate=cost,
        compiler_params=pltpu.CompilerParams(vmem_limit_bytes=limit * 1024 * 1024),
    )


def shards(queries, key_tokens, values, position_bias, out_weight):
    width = queries.shape[3]
    rows, cols = ("z", "xl", "core"), ("xh", "y")
    nr, nc = lax.axis_size(rows), lax.axis_size(cols)
    r, c = lax.axis_index(rows), lax.axis_index(cols)

    down = [(n, (n + 1) % nr) for n in range(nr)]
    up = [(n, (n - 1) % nr) for n in range(nr)]
    right = [(n, (n + 1) % nc) for n in range(nc)]
    left = [(n, (n - 1) % nc) for n in range(nc)]
    k, v, q = (a.reshape(64, width) for a in (key_tokens, values, queries))
    packed = call(weight_kernel, jax.ShapeDtypeStruct((16, 72, 128), BF), 1, limit=4)(out_weight.T)
    along_zx = lax.all_to_all(packed, ("xh", "z"), 0, 0, tiled=True)

    both = jnp.stack([k, v], 0)
    to_down, to_up = both[:, 16:], both[:, :48]
    top = lax.ppermute(to_down, rows, down).reshape(96, width)
    bot = lax.ppermute(to_up, rows, up).reshape(96, width)
    side = jax.ShapeDtypeStruct((64, width), BF)
    to_left, to_right = call(pack_kernel, (side, side), 4, flops=50000000000)(to_up, to_down, top, bot)
    from_left = lax.ppermute(to_right, cols, right)
    from_right = lax.ppermute(to_left, cols, left)

    near = along_zx.reshape(2, 8, 72, 128)
    stages = [near] + [lax.ppermute(near, "y", [(n, n ^ k) for n in range(4)]) for k in (1, 3, 2)]

    place = jnp.stack([r * 4, c * 16, nr * 4, nc * 16]).astype(jnp.int32)
    bias = jnp.pad(position_bias, ((0, 0), (0, 128 - 49)), constant_values=-jnp.inf)
    mixed = call(attention_kernel, side, 9, smem=(0,), flops=50000000000)(
        place, q, k, v, top, bot, from_left, from_right, bias
    )
    swap = [(0, 1), (1, 0)]
    next_mixed = lax.ppermute(mixed, "xl", swap)
    core_mixed = lax.ppermute(mixed, "core", swap)
    both_mixed = lax.ppermute(next_mixed, "core", swap)
    weights = call(unpack_kernel, jax.ShapeDtypeStruct((8, 384, 192), BF), 4, flops=100000000000)(*stages)
    part = jax.ShapeDtypeStruct((64, width // 4), BF)
    y = lax.axis_index("y").astype(jnp.int32).reshape(1)
    keep, to_chip, to_core, to_both = call(project_kernel, (part,) * 4, 6, smem=(0,))(
        y, mixed, next_mixed, core_mixed, both_mixed, weights
    )
    by_core = lax.ppermute(to_core, "core", swap)
    by_chip = lax.ppermute(to_chip, "xl", swap)
    by_both = lax.ppermute(to_both, ("xl", "core"), [(n, 3 - n) for n in range(4)])
    at = jnp.stack([lax.axis_index("xl"), lax.axis_index("core")]).astype(jnp.int32)
    out = call(assemble_kernel, side, 5, smem=(0,))(at, keep, by_core, by_chip, by_both)
    return out.reshape(queries.shape)


def solution(mesh):
    fine = Mesh(mesh.devices.reshape(8, 2, 2, 2, 4), ("z", "xl", "core", "xh", "y"))
    rows, cols = ("z", "xl", "core"), ("xh", "y")
    tokens = P(None, rows, cols, None)
    return jax.shard_map(
        shards,
        mesh=fine,
        in_specs=(tokens, tokens, tokens, P(), P(cols, rows)),
        out_specs=tokens,
        check_vma=False,
    )
```

```python
import jax
import jax.numpy as jnp
from jax import lax
from jax.experimental import pallas as pl
from jax.experimental.pallas import tpu as pltpu
from jax.sharding import Mesh, PartitionSpec as P

VM = pl.BlockSpec(memory_space=pltpu.VMEM)
SM = pl.BlockSpec(memory_space=pltpu.SMEM)
BF = jnp.bfloat16
F32 = jnp.float32
NT = (((1,), (1,)), ((), ()))


def weight_kernel(wt_ref, out_ref):
    w = wt_ref[...]
    packed = jnp.concatenate([w[:, :128], jnp.concatenate([w[:24, 128:], w[24:, 128:]], 1)], 0)
    for n in range(out_ref.shape[0]):
        out_ref[n] = packed


def pack_kernel(up_ref, down_ref, top_ref, bot_ref, left_ref, right_ref):
    i = lax.broadcasted_iota(jnp.int32, (64, 160), 0)
    source = lax.broadcasted_iota(jnp.int32, (64, 160), 1)
    t = i & 31
    r = (t * 171) >> 9
    x = t - r * 3 + (i >> 5) * 13
    start = jnp.where(r < 3, r * 16 + 64, jnp.where(r < 7, r * 16 - 48, r * 16))
    pick = jnp.where((source == start + x) & (t < 30), 1.0, 0.0).astype(BF)
    for n in range(2):
        tokens = jnp.concatenate(
            [up_ref[n], down_ref[n, 32:, :], top_ref[n * 48 : n * 48 + 48, :], bot_ref[n * 48 : n * 48 + 48, :]], 0
        )
        got = jnp.dot(pick, tokens, preferred_element_type=F32).astype(BF)
        left_ref[n * 32 : n * 32 + 32, :] = got[:32]
        right_ref[n * 32 : n * 32 + 32, :] = got[32:]


def attention_kernel(
    place_ref, q_ref, k_ref, v_ref, top_ref, bot_ref, left_ref, right_ref, bias_ref, o_ref
):
    heads = bias_ref.shape[0]
    shape = (64, 256)
    i = lax.broadcasted_iota(jnp.int32, shape, 0)
    j = lax.broadcasted_iota(jnp.int32, shape, 1)
    y, x = i >> 4, i & 15
    side = j & 31
    side_row = ((side * 171) >> 9) - 3
    side_col = side - (side_row + 3) * 3
    ky = jnp.where(
        j < 64,
        j >> 4,
        jnp.where(j < 112, (j >> 4) - 7, jnp.where(j < 160, (j >> 4) - 3, side_row)),
    )
    kx = jnp.where(j < 160, j & 15, jnp.where(j < 192, side_col - 3, side_col + 16))
    dy, dx = ky - y + 3, kx - x + 3
    gy, gx = ky + place_ref[0], kx + place_ref[1]
    inside = (dy >= 0) & (dy < 7) & (dx >= 0) & (dx < 7)
    inside = inside & (gy >= 0) & (gy < place_ref[2]) & (gx >= 0) & (gx < place_ref[3])
    inside = inside & ((j < 160) | (side < 30)) & (j < 224)
    code = jnp.where(inside, dy * 7 + dx, 127)
    code_low, code_high = code[:, :128], code[:, 128:]
    low = lax.broadcasted_iota(jnp.int32, (64, 128), 1) < 64
    zeros = jnp.zeros((32, 128), BF)
    none = jnp.zeros((64, 128), BF)

    for pair in range(heads // 2):
        c = slice(pair * 128, pair * 128 + 128)
        q = q_ref[:, c]
        q2 = jnp.concatenate([jnp.where(low, q, none), jnp.where(low, none, q)], 0)
        keys = jnp.concatenate(
            [k_ref[:, c], top_ref[:48, c], bot_ref[:48, c], left_ref[:32, c], right_ref[:32, c], zeros], 0
        )
        vals = jnp.concatenate(
            [v_ref[:, c], top_ref[48:, c], bot_ref[48:, c], left_ref[32:, c], right_ref[32:, c], zeros], 0
        )
        s = lax.dot_general(q2, keys, NT, preferred_element_type=F32)
        bias = []
        for h in (2 * pair, 2 * pair + 1):
            row = jnp.broadcast_to(bias_ref[h : h + 1, :], (64, 128))
            bias.append(
                jnp.concatenate(
                    [
                        jnp.take_along_axis(row, code_low, axis=1, mode="promise_in_bounds"),
                        jnp.take_along_axis(row, code_high, axis=1, mode="promise_in_bounds"),
                    ],
                    1,
                )
            )
        s = s * 0.125 + jnp.concatenate(bias, 0)
        e = jnp.exp(s - jnp.max(s, 1, keepdims=True))
        p = (e * (1.0 / jnp.sum(e, 1, keepdims=True))).astype(BF)
        o = jnp.dot(p, vals, preferred_element_type=F32)
        o_ref[:, c] = jnp.where(low, o[:64], o[64:]).astype(BF)


def unpack_kernel(w0_ref, w3_ref, w1_ref, w2_ref, out_ref):
    for xh in range(2):
        for k, w_ref in enumerate((w0_ref, w1_ref, w2_ref, w3_ref)):
            for z in range(8):
                w = w_ref[xh, z]
                tail = w[48:]
                tail = jnp.concatenate([tail[:, :64], tail[:, 64:]], 0)
                out_ref[xh * 4 + k, z * 48 : z * 48 + 48, :] = jnp.concatenate([w[:48], tail], 1)


def project_kernel(y_ref, a_ref, b_ref, c_ref, d_ref, w_ref, keep_ref, chip_ref, core_ref, both_ref):
    mixed = jnp.concatenate([a_ref[...], b_ref[...], c_ref[...], d_ref[...]], 0)
    odd, upper = (y_ref[0] & 1) == 1, y_ref[0] >= 2
    total = None
    for xh in range(2):
        f = [mixed[:, xh * 768 + n * 192 : xh * 768 + n * 192 + 192] for n in range(4)]
        f = [jnp.where(odd, f[n ^ 1], f[n]) for n in range(4)]
        f = [jnp.where(upper, f[n ^ 2], f[n]) for n in range(4)]
        for k in range(4):
            term = lax.dot_general(f[k], w_ref[xh * 4 + k], NT, preferred_element_type=F32)
            total = term if total is None else total + term
    out = total.astype(BF)
    for n, ref in enumerate((keep_ref, chip_ref, core_ref, both_ref)):
        ref[...] = out[n * 64 : n * 64 + 64]


def assemble_kernel(at_ref, keep_ref, core_ref, chip_ref, both_ref, o_ref):
    parts = (keep_ref, core_ref, chip_ref, both_ref)
    for me in range(4):

        @pl.when(at_ref[0] * 2 + at_ref[1] == me)
        def _():
            quarters = [parts[me ^ q][...] for q in range(4)]
            pieces = [part[:, n * 48 : n * 48 + 48] for n in range(8) for part in quarters]
            o_ref[...] = jnp.concatenate(pieces, 1)


def call(kernel, outs, n_in, smem=(), limit=48, flops=0):
    cost = pl.CostEstimate(flops=flops, bytes_accessed=4 * 1024 * 1024, transcendentals=0) if flops else None
    return pl.pallas_call(
        kernel,
        out_shape=outs,
        in_specs=[SM if k in smem else VM for k in range(n_in)],
        out_specs=VM if isinstance(outs, jax.ShapeDtypeStruct) else tuple(VM for _ in outs),
        cost_estimate=cost,
        compiler_params=pltpu.CompilerParams(vmem_limit_bytes=limit * 1024 * 1024),
    )


def shards(queries, key_tokens, values, position_bias, out_weight):
    width = queries.shape[3]
    rows, cols = ("z", "xl", "core"), ("xh", "y")
    nr, nc = lax.axis_size(rows), lax.axis_size(cols)
    r, c = lax.axis_index(rows), lax.axis_index(cols)

    down = [(n, (n + 1) % nr) for n in range(nr)]
    up = [(n, (n - 1) % nr) for n in range(nr)]
    right = [(n, (n + 1) % nc) for n in range(nc)]
    left = [(n, (n - 1) % nc) for n in range(nc)]
    k, v, q = (a.reshape(64, width) for a in (key_tokens, values, queries))
    packed = call(weight_kernel, jax.ShapeDtypeStruct((16, 72, 128), BF), 1, limit=4)(out_weight.T)
    along_zx = lax.all_to_all(packed, ("xh", "z"), 0, 0, tiled=True)

    both = jnp.stack([k, v], 0)
    to_down, to_up = both[:, 16:], both[:, :48]
    top = lax.ppermute(to_down, rows, down).reshape(96, width)
    bot = lax.ppermute(to_up, rows, up).reshape(96, width)
    side = jax.ShapeDtypeStruct((64, width), BF)
    to_left, to_right = call(pack_kernel, (side, side), 4, flops=50000000000)(to_up, to_down, top, bot)
    from_left = lax.ppermute(to_right, cols, right)
    from_right = lax.ppermute(to_left, cols, left)

    near = along_zx.reshape(2, 8, 72, 128)
    stages = [near] + [lax.ppermute(near, "y", [(n, n ^ k) for n in range(4)]) for k in (3, 1, 2)]

    place = jnp.stack([r * 4, c * 16, nr * 4, nc * 16]).astype(jnp.int32)
    bias = jnp.pad(position_bias, ((0, 0), (0, 128 - 49)), constant_values=-jnp.inf)
    mixed = call(attention_kernel, side, 9, smem=(0,), flops=50000000000)(
        place, q, k, v, top, bot, from_left, from_right, bias
    )
    swap = [(0, 1), (1, 0)]
    next_mixed = lax.ppermute(mixed, "xl", swap)
    core_mixed = lax.ppermute(mixed, "core", swap)
    both_mixed = lax.ppermute(next_mixed, "core", swap)
    weights = call(unpack_kernel, jax.ShapeDtypeStruct((8, 384, 192), BF), 4, flops=100000000000)(*stages)
    part = jax.ShapeDtypeStruct((64, width // 4), BF)
    y = lax.axis_index("y").astype(jnp.int32).reshape(1)
    keep, to_chip, to_core, to_both = call(project_kernel, (part,) * 4, 6, smem=(0,))(
        y, mixed, next_mixed, core_mixed, both_mixed, weights
    )
    by_core = lax.ppermute(to_core, "core", swap)
    by_chip = lax.ppermute(to_chip, "xl", swap)
    by_both = lax.ppermute(to_both, ("xl", "core"), [(n, 3 - n) for n in range(4)])
    at = jnp.stack([lax.axis_index("xl"), lax.axis_index("core")]).astype(jnp.int32)
    out = call(assemble_kernel, side, 5, smem=(0,))(at, keep, by_core, by_chip, by_both)
    return out.reshape(queries.shape)


def solution(mesh):
    fine = Mesh(mesh.devices.reshape(8, 2, 2, 2, 4), ("z", "xl", "core", "xh", "y"))
    rows, cols = ("z", "xl", "core"), ("xh", "y")
    tokens = P(None, rows, cols, None)
    return jax.shard_map(
        shards,
        mesh=fine,
        in_specs=(tokens, tokens, tokens, P(), P(cols, rows)),
        out_specs=tokens,
        check_vma=False,
    )
```
